256 devices in a mesh: shot: 64 (over z, x_lo, y), rcv: 4 (over x_hi, core).
Axes of the slice: x: 4 (x_hi: 2, x_lo: 2; x = x_hi * 2 + x_lo), y: 4, z: 8, core: 2. Of those that a mesh axis runs over, the one named last changes fastest.
Arguments:
- records: bfloat16 [1, 2, 8192, 8192], P(None, None, 'shot', 'rcv'), may hold values from -6 to 6
- aperture: int32 [8192, 2], P('shot'), may hold values from 0 to 3, all different within a row
- block_owner: int32 [4], replicated, may hold values from 0 to 63, as said below
- block_receivers: int32 [4, 128], replicated, may hold values from 0 to 8191, as said below
Outputs:
- multiples: bfloat16 [1, 2, 8192, 8192], P(None, None, 'shot', 'rcv')
The draws below stay inside these ranges and needn't reach their ends.
Inputs may be any that keep to these rules, and one draw needn't show every extreme that they name: `block_owner`: distinct indices. `block_receivers`: distinct receivers.
All inputs are finite; a program needn't handle non-finite values.
Results may differ from the reference program's by a relative error of at most 0.001.
Values may be sent and summed in bfloat16 or wider, within the bound.
A program may use at most 128 MiB of HBM per device.

```python
import jax
import jax.numpy as jnp
from jax import lax

F = 1
SH_DEV = 128
RCV = 8192
NBLK = 4
APER = 2
BLOCK = 128
SHOTS = 8192
N_SHOT = 64


def draw_block_owner(key, part):
    middle = jax.random.permutation(jax.random.fold_in(key, 11), N_SHOT - 2)[:NBLK - 2] + 1
    ends = jnp.array([0, N_SHOT - 1], dtype=jnp.int32)
    owners = jnp.concatenate([ends, middle.astype(jnp.int32)])
    placing = jax.random.permutation(jax.random.fold_in(key, 13), NBLK)
    return owners[placing].astype(jnp.int32)


def draw_block_receivers(key, part):
    middle = jax.random.permutation(jax.random.fold_in(key, 23), RCV - 2)[:NBLK * BLOCK - 2] + 1
    ends = jnp.array([0, RCV - 1], dtype=jnp.int32)
    chosen = jnp.concatenate([ends, middle.astype(jnp.int32)])
    placing = jax.random.permutation(jax.random.fold_in(key, 29), NBLK * BLOCK)
    return chosen[placing].reshape(NBLK, BLOCK).astype(jnp.int32)


def levels(key, extent, shards, smallest, high):
    factor_of = 1.0
    for position, shards_of in shards:
        heights = jax.random.uniform(jax.random.fold_in(jax.random.fold_in(key, 6), position), (shards_of,), jnp.float32, smallest / len(shards), high / len(shards))
        factor_of = factor_of * jnp.repeat(jnp.exp(heights), extent[position] // shards_of).reshape((-1,) + (1,) * (len(extent) - 1 - position))
    return factor_of


def different_ones(key, rows, amount, top, lift):
    order = jax.random.permutation(jax.random.fold_in(key, 1), amount)
    pull = order
    for power in range(3):
        pull = pull * pull // amount
    pull = pull * lift // amount
    chance = jax.random.randint(jax.random.fold_in(key, 2), (rows, amount), 0, 4096) + pull
    sure = jax.random.permutation(jax.random.fold_in(key, 3), rows)[jnp.arange(amount) % rows]
    chance = jnp.where(jnp.arange(rows)[:, None] == sure[None, :], 1 << 14, chance)
    score = chance * amount + jnp.arange(amount)
    return lax.top_k(score.astype(jnp.int32), top)[1].astype(jnp.int32)


def gaussian(key, extent, scale, limit, cuts=(), kind=jnp.bfloat16):
    values = scale * jax.random.normal(key, extent, jnp.float32)
    if cuts:
        values = values * levels(key, extent, cuts, -0.22, 0.18)
    return jnp.clip(values, -limit, limit).astype(kind)


def setup_inputs(seed: int = 0) -> dict:
    seeds = jax.random.split(jax.random.key(seed), 5)
    records = gaussian(seeds[0], (F, 2, SHOTS, RCV), 1.0, 6.0, ((2, 64), (3, 4)))
    aperture = different_ones(seeds[1], SHOTS, NBLK, APER, 8192)
    block_owner = draw_block_owner(jax.random.fold_in(seeds[4], 71), 0)
    block_receivers = draw_block_receivers(jax.random.fold_in(seeds[4], 71), 0)
    return {"records": records, "aperture": aperture, "block_owner": block_owner, "block_receivers": block_receivers}


def reference(records, aperture, block_owner, block_receivers):
    cols = block_receivers.reshape(-1).astype(jnp.int32)
    near = jnp.take(records, cols, axis=3)
    blocks = jnp.arange(NBLK, dtype=jnp.int32)
    use = jnp.any(aperture[:, :, None] == blocks[None, None, :], axis=1)
    near = near.reshape(F, 2, SHOTS, NBLK, BLOCK) * use[None, None, :, :, None].astype(near.dtype)
    near = near.reshape(F, 2, SHOTS, NBLK * BLOCK).astype(jnp.float32)
    real_total = jnp.zeros((F, SHOTS, RCV), jnp.float32)
    imaginary_total = jnp.zeros((F, SHOTS, RCV), jnp.float32)
    for block in range(NBLK):
        start = (block_owner[block] * SH_DEV).astype(jnp.int32)
        distant_offset = lax.dynamic_slice_in_dim(records, start, SH_DEV, axis=2).astype(jnp.float32)
        block_portion = near[:, :, :, block * BLOCK:(block + 1) * BLOCK]
        real_total = real_total + jnp.einsum('uze,uew->uzw', block_portion[:, 0], distant_offset[:, 0]) - jnp.einsum('uze,uew->uzw', block_portion[:, 1], distant_offset[:, 1])
        imaginary_total = imaginary_total + jnp.einsum('uze,uew->uzw', block_portion[:, 0], distant_offset[:, 1]) + jnp.einsum('uze,uew->uzw', block_portion[:, 1], distant_offset[:, 0])
    factor = (2.0 * APER * BLOCK) ** -0.5
    return (jnp.stack([real_total, imaginary_total], axis=1) * factor).astype(jnp.bfloat16)
```

```python
import functools

import jax
import jax.numpy as jnp
from jax import lax
from jax.experimental import pallas as pl
from jax.experimental.pallas import tpu as pltpu
from jax.sharding import PartitionSpec as P

MESH = pl.DeviceIdType.MESH
BF16 = jnp.bfloat16
APER = 2
BLOCK = 128
NBLK = 4
NX, NY, NZ, NR = 2, 4, 8, 4
NQ = NX * NY
SHARE = 256
NC = 2
LANES = SHARE // NC
ROWS = 2 * BLOCK
SUB = ROWS // NZ


def remote(src, dst, send_sem, recv_sem, device):
    return pltpu.make_async_remote_copy(
        src_ref=src, dst_ref=dst, send_sem=send_sem, recv_sem=recv_sem, device_id=device, device_id_type=MESH
    )


def kernel(
    rec, aperture, owner, receivers, out,
    scat0, scat1, zscat0, zscat1, sel, part, gath, far, near, local, given, stage,
    s1s, s1r, s2s, s2r, s3s, s3r, n1s, n1r, n2s, n2r, n3s, n3r, os, orr,
):
    scat, zscat = (scat0, scat1), (zscat0, zscat1)
    shot, r = lax.axis_index("shot"), lax.axis_index("rcv")
    z, q = shot // NQ, lax.rem(shot, NQ)
    core = lax.rem(r, 2)
    other_core = (shot, r + 1 - 2 * core)
    other_x = (shot, lax.rem(r + 2, NR))

    def plane(d):
        index = lax.rem(q + d, NQ)
        return index, (z * NQ + index, r)

    def line(d):
        index = lax.rem(z + d, NZ)
        return index, (index * NQ + q, r)

    barrier = pltpu.get_barrier_semaphore()
    for d in range(1, NQ):
        pl.semaphore_signal(barrier, inc=1, device_id=plane(d)[1], device_id_type=MESH)
    for d in range(1, NZ):
        pl.semaphore_signal(barrier, inc=1, device_id=line(d)[1], device_id_type=MESH)
    pl.semaphore_signal(barrier, inc=1, device_id=other_core, device_id_type=MESH)
    pl.semaphore_signal(barrier, inc=1, device_id=other_x, device_id_type=MESH)
    pl.semaphore_wait(barrier, NQ - 1 + NZ - 1 + 2)

    def columns(index, n):
        return pl.ds(pl.multiple_of(index * SHARE + n * LANES, LANES), LANES)

    def s1(n, d, source):
        index, device = plane(d)
        return remote(
            rec.at[:, columns(index, n)], scat[n].at[source], s1s.at[n, d], s1r.at[n, source], device
        )

    def s2(n, d, source):
        index, device = line(d)
        return remote(sel.at[n, index], zscat[n].at[source], s2s.at[n, d], s2r.at[n, source], device)

    def s3(n, d, source):
        index, device = line(d)
        return remote(part.at[n], gath.at[n, source], s3s.at[n, d], s3r.at[n, source], device)

    def o(n, d, source):
        index, device = plane(d)
        return remote(
            stage.at[n, index], out.at[:, columns(source, n)], os.at[n, d], orr.at[n, source], device
        )

    def n2(d, source):
        index, device = plane(d)
        return remote(
            near.at[q, core], near.at[source, core], n2s.at[d], n2r.at[source], device
        )

    def n3(index, half):
        return remote(near.at[index, half], near.at[index, half], n3s.at[index], n3r.at[index], other_core)

    for n in range(NC):
        for d in range(1, NQ):
            s1(n, d, q).start()
    for n in range(NC):
        scat[n][q] = rec[:, columns(q, n)]

    first = r * (NQ * SHARE)
    points = jnp.concatenate([receivers[b : b + 1, :] for b in range(NBLK)], axis=1)
    tile = 256
    total = jnp.zeros((ROWS, NBLK * BLOCK), jnp.float32)
    for k in range(NQ * SHARE // tile):
        ids = first + k * tile + lax.broadcasted_iota(jnp.int32, (tile, NBLK * BLOCK), 0)
        chosen = jnp.where(ids == points, 1.0, 0.0).astype(BF16)
        total += jnp.dot(rec[:, k * tile : (k + 1) * tile], chosen, preferred_element_type=jnp.float32)
    block = lax.broadcasted_iota(jnp.int32, (BLOCK, NBLK * BLOCK), 1) // BLOCK
    use = (block == aperture[:, 0:1]) | (block == aperture[:, 1:2])
    for c in range(2):
        local[c] = jnp.where(use, total[c * BLOCK : (c + 1) * BLOCK], 0.0).astype(BF16)

    n1a = remote(local.at[1 - core], given.at[0], n1s.at[0], n1r.at[0], other_core)
    n1a.start()
    n1a.wait_recv()
    given[2] = local[core] + given[0]
    n1b = remote(given.at[2], given.at[1], n1s.at[1], n1r.at[1], other_x)
    n1b.start()

    zb = [owner[b] // NQ for b in range(NBLK)]
    qb = [lax.rem(owner[b], NQ) for b in range(NBLK)]

    def to_line(n):
        for d in range(1, NQ):
            source = lax.rem(q + d, NQ)
            s1(n, d, source).wait_recv()
        for b in range(NBLK):
            piece = scat[n][qb[b]]
            for k in range(NZ):
                sel[n, k, b] = piece[k * SUB : (k + 1) * SUB]
        for d in range(1, NZ):
            s2(n, d, z).start()
        zscat[n][z] = sel[n, z]

    def gather_line(n):
        for d in range(1, NZ):
            s2(n, d, lax.rem(z + d, NZ)).wait_recv()
        for b in range(NBLK):
            part[n, b] = zscat[n][zb[b], b]
        for d in range(1, NZ):
            s3(n, d, z).start()
        gath[n, z] = part[n]

    to_line(0)
    n1b.wait_recv()
    near[q, core] = given[1] + given[2]
    for d in range(1, NQ):
        n2(d, q).start()
    n3(q, core).start()
    to_line(1)
    gather_line(0)
    gather_line(1)
    for d in range(1, NQ):
        source = lax.rem(q + d, NQ)
        n2(d, source).wait_recv()
        n3(source, core).start()
    for d in range(NQ):
        n3(lax.rem(q + d, NQ), 1 - core).wait_recv()

    factor = (2.0 * APER * BLOCK) ** (-0.5)
    half = NZ // 2
    for n in range(NC):
        for d in range(1, NZ):
            s3(n, d, lax.rem(z + d, NZ)).wait_recv()
        for k in range(NZ):
            for b in range(NBLK):
                start = b * BLOCK + (k % half) * SUB
                far[n, k // half, start : start + SUB] = gath[n, k, b]

        def product(index):
            rows = near[index].reshape(ROWS, NBLK * BLOCK)
            by_real = jnp.dot(rows, far[n, 0], preferred_element_type=jnp.float32)
            by_imag = jnp.dot(rows, far[n, 1], preferred_element_type=jnp.float32)
            real = by_real[:BLOCK] - by_imag[BLOCK:]
            imag = by_real[BLOCK:] + by_imag[:BLOCK]
            return (jnp.concatenate([real, imag], axis=0) * factor).astype(BF16)

        for d in range(1, NQ):
            index = lax.rem(q + d, NQ)
            stage[n, index] = product(index)
            o(n, d, q).start()
        out[:, columns(q, n)] = product(q)

    for n in range(NC):
        for d in range(1, NQ):
            o(n, d, lax.rem(q + d, NQ)).wait_recv()
    n1a.wait_send()
    n1b.wait_send()
    for d in range(1, NQ):
        n2(d, q).wait_send()
    for index in range(NQ):
        n3(index, core).wait_send()
    for n in range(NC):
        for d in range(1, NQ):
            s1(n, d, q).wait_send()
            o(n, d, q).wait_send()
        for d in range(1, NZ):
            s2(n, d, z).wait_send()
            s3(n, d, z).wait_send()


def per_device(records, aperture, block_owner, block_receivers):
    freqs, parts, shots_here, rcv_here = records.shape
    vmem = pl.BlockSpec(memory_space=pltpu.VMEM)
    dma = pltpu.SemaphoreType.DMA
    out = pl.pallas_call(
        kernel,
        out_shape=jax.ShapeDtypeStruct((ROWS, rcv_here), BF16),
        in_specs=[vmem, vmem, pl.BlockSpec(memory_space=pltpu.SMEM), vmem],
        out_specs=vmem,
        scratch_shapes=[
            pltpu.VMEM((NQ, ROWS, LANES), BF16),
            pltpu.VMEM((NQ, ROWS, LANES), BF16),
            pltpu.VMEM((NZ, NBLK, SUB, LANES), BF16),
            pltpu.VMEM((NZ, NBLK, SUB, LANES), BF16),
            pltpu.VMEM((NC, NZ, NBLK, SUB, LANES), BF16),
            pltpu.VMEM((NC, NBLK, SUB, LANES), BF16),
            pltpu.VMEM((NC, NZ, NBLK, SUB, LANES), BF16),
            pltpu.VMEM((NC, 2, NBLK * BLOCK, LANES), BF16),
            pltpu.VMEM((NQ, 2, BLOCK, NBLK * BLOCK), BF16),
            pltpu.VMEM((2, BLOCK, NBLK * BLOCK), BF16),
            pltpu.VMEM((3, BLOCK, NBLK * BLOCK), BF16),
            pltpu.VMEM((NC, NQ, ROWS, LANES), BF16),
            dma((NC, NQ)), dma((NC, NQ)),
            dma((NC, NZ)), dma((NC, NZ)),
            dma((NC, NZ)), dma((NC, NZ)),
            dma((2,)), dma((2,)),
            dma((NQ,)), dma((NQ,)),
            dma((NQ,)), dma((NQ,)),
            dma((NC, NQ)), dma((NC, NQ)),
        ],
        compiler_params=pltpu.CompilerParams(
            collective_id=0, has_side_effects=True, vmem_limit_bytes=48 * 1024 * 1024
        ),
        cost_estimate=pl.CostEstimate(flops=2 * 10**9, bytes_accessed=2 * 2**20, transcendentals=0),
    )(records.reshape(ROWS, rcv_here), aperture, block_owner, block_receivers)
    return out.reshape(freqs, parts, shots_here, rcv_here)


def solution(mesh):
    placed = (P(None, None, "shot", "rcv"), P("shot", None), P(), P())
    return jax.shard_map(
        per_device,
        mesh=mesh,
        in_specs=placed,
        out_specs=P(None, None, "shot", "rcv"),
        check_vma=False,
    )
```

```python
import jax
import jax.numpy as jnp
from jax import lax
from jax.experimental import pallas as pl
from jax.experimental.pallas import tpu as pltpu
from jax.sharding import PartitionSpec as P

MESH = pl.DeviceIdType.MESH
BF16 = jnp.bfloat16
F32 = jnp.float32
APER = 2
BLOCK = 128
NBLK = 4
NX, NY, NZ, NR = 2, 4, 8, 4
NQ = NX * NY
SHARE = 256
NC = 2
LANES = SHARE // NC
ROWS = 2 * BLOCK
SUB = BLOCK // NZ
WIDTH = APER * BLOCK
TAIL = 16
SHIFT = (1, NZ - 1)


def remote(src, dst, send_sem, recv_sem, device):
    return pltpu.make_async_remote_copy(
        src_ref=src, dst_ref=dst, send_sem=send_sem, recv_sem=recv_sem, device_id=device, device_id_type=MESH
    )


def kernel(
    rec_hbm, ap_hbm, owner_hbm, recv_hbm, out,
    rec, ap, receivers, owner,
    scat0, scat1, zscat0, zscat1, sel, part, gath, far, near, local, given, lhs, stage,
    ins, s1s, s1r, s2s, s2r, s3s, s3r, n1s, n1r, n2s, n2r, n3s, n3r, os, orr,
):
    scat, zscat = (scat0, scat1), (zscat0, zscat1)
    shot, r = lax.axis_index("shot"), lax.axis_index("rcv")
    z, q = shot // NQ, lax.rem(shot, NQ)
    core = lax.rem(r, 2)
    other_core = (shot, r + 1 - 2 * core)
    other_x = (shot, lax.rem(r + 2, NR))

    inputs = [
        pltpu.make_async_copy(src, dst, ins.at[k])
        for k, (src, dst) in enumerate(((rec_hbm, rec), (ap_hbm, ap), (recv_hbm, receivers), (owner_hbm, owner)))
    ]
    for copy in inputs:
        copy.start()

    def at(index, plane):
        return (plane * NQ + index, r)

    def plane(d):
        index = lax.rem(q + d, NQ)
        return index, at(index, z)

    def line(d):
        index = lax.rem(z + d, NZ)
        return index, at(q, index)

    barrier = pltpu.get_barrier_semaphore()
    for d in range(1, NQ):
        index = lax.rem(q + d, NQ)
        for plane_of in (z, *(lax.rem(z + shift, NZ) for shift in SHIFT)):
            pl.semaphore_signal(barrier, inc=1, device_id=at(index, plane_of), device_id_type=MESH)
    for d in range(1, NZ):
        pl.semaphore_signal(barrier, inc=1, device_id=line(d)[1], device_id_type=MESH)
    pl.semaphore_signal(barrier, inc=1, device_id=other_core, device_id_type=MESH)
    pl.semaphore_signal(barrier, inc=1, device_id=other_x, device_id_type=MESH)
    pl.semaphore_wait(barrier, 3 * (NQ - 1) + NZ - 1 + 2)

    def columns(index, n):
        return pl.ds(pl.multiple_of(index * SHARE + n * LANES, LANES), LANES)

    def s1(n, e, d, source):
        index = lax.rem(q + d, NQ)
        return remote(
            rec_hbm.at[pl.ds(e * BLOCK, BLOCK), columns(index, n)], scat[n].at[e, source],
            s1s.at[n, e, d], s1r.at[n, e, source], at(index, lax.rem(z + e * SHIFT[n], NZ)),
        )

    def s2(n, d, source):
        index, device = line(d)
        return remote(sel.at[n, index], zscat[n].at[source], s2s.at[n, d], s2r.at[n, source], device)

    def s3(n, d, source):
        return remote(part.at[n], gath.at[n, source], s3s.at[n, d], s3r.at[n, source], line(d)[1])

    def o(n, d, source):
        index, device = plane(d)
        return remote(stage.at[n, index], out.at[:, columns(source, n)], os.at[n, d], orr.at[n, source], device)

    def n2(d, source):
        return remote(near.at[q, core], near.at[source, core], n2s.at[d], n2r.at[source], plane(d)[1])

    def n3(index, half):
        return remote(near.at[index, half], near.at[index, half], n3s.at[index], n3r.at[index], other_core)

    offsets = [[(e, d) for d in range(NQ) for e in (1, 0) if (e, d) != (0, 0)]] * NC
    for n in range(NC):
        for e, d in offsets[n]:
            s1(n, e, d, q).start()
    for copy in inputs:
        copy.wait()
    for n in range(NC):
        scat[n][0, q] = rec[:BLOCK, columns(q, n)]

    first = r * (NQ * SHARE)
    points = jnp.concatenate([receivers[b : b + 1, :] for b in range(NBLK)], axis=1)
    tile = 256
    total = jnp.zeros((ROWS, NBLK * BLOCK), F32)
    for k in range(NQ * SHARE // tile):
        ids = first + k * tile + lax.broadcasted_iota(jnp.int32, (tile, NBLK * BLOCK), 0)
        chosen = jnp.where(ids == points, 1.0, 0.0).astype(BF16)
        total += jnp.dot(rec[:, k * tile : (k + 1) * tile], chosen, preferred_element_type=F32)
    diagonal = lax.broadcasted_iota(jnp.int32, (BLOCK, BLOCK), 0) == lax.broadcasted_iota(
        jnp.int32, (BLOCK, BLOCK), 1
    )

    def upright(row):
        return jnp.sum(jnp.where(diagonal, row, 0.0), axis=1, keepdims=True)

    apertures = ap[...].astype(F32)
    for a in range(APER):
        block = upright(apertures[a : a + 1])
        for c in range(2):
            rows = total[c * BLOCK : (c + 1) * BLOCK]
            found = rows[:, :BLOCK]
            for b in range(1, NBLK):
                found = jnp.where(block == b, rows[:, b * BLOCK : (b + 1) * BLOCK], found)
            local[c, :, a * BLOCK : (a + 1) * BLOCK] = found.astype(BF16)

    n1a = remote(local.at[1 - core], given.at[0], n1s.at[0], n1r.at[0], other_core)
    n1a.start()
    tail = jnp.concatenate([apertures[a : a + 1] for a in range(APER)], axis=1)
    near[q, core, BLOCK:] = jnp.broadcast_to(tail, (TAIL, WIDTH)).astype(BF16)
    n1a.wait_recv()
    given[2] = local[core] + given[0]
    n1b = remote(given.at[2], given.at[1], n1s.at[1], n1r.at[1], other_x)
    n1b.start()

    zb = [owner[b] // NQ for b in range(NBLK)]
    qb = [lax.rem(owner[b], NQ) for b in range(NBLK)]

    def to_line(n):
        for e, d in offsets[n]:
            s1(n, e, d, lax.rem(q + d, NQ)).wait_recv()
        for b in range(NBLK):
            piece = scat[n][jnp.where(zb[b] == z, 0, 1), qb[b]]
            for k in range(NZ):
                sel[n, k, b] = piece[k * SUB : (k + 1) * SUB]
        for d in range(1, NZ):
            s2(n, d, z).start()
        zscat[n][z] = sel[n, z]

    def gather_line(n):
        for d in range(1, NZ):
            s2(n, d, lax.rem(z + d, NZ)).wait_recv()
        for b in range(NBLK):
            for c in range(2):
                part[n, b, c] = zscat[n][lax.rem(zb[b] + c * SHIFT[n], NZ), b]
        for d in range(1, NZ):
            s3(n, d, z).start()
        gath[n, z] = part[n]

    to_line(0)
    n1b.wait_recv()
    near[q, core, :BLOCK] = given[1] + given[2]
    for d in range(1, NQ):
        n2(d, q).start()
    n3(q, core).start()
    to_line(1)
    gather_line(0)
    gather_line(1)
    for d in range(1, NQ):
        source = lax.rem(q + d, NQ)
        n2(d, source).wait_recv()
        n3(source, core).start()
    for d in range(NQ):
        index = lax.rem(q + d, NQ)
        n3(index, 1 - core).wait_recv()
        tail = near[index, 0, BLOCK:].astype(F32)
        blocks = [upright(tail[:1, a * BLOCK : (a + 1) * BLOCK]) for a in range(APER)]
        for b in range(NBLK):
            use = [(block == b).astype(F32).astype(BF16) for block in blocks]
            for c in range(2):
                lhs[index, c, :, b * BLOCK : (b + 1) * BLOCK] = (
                    near[index, c, :BLOCK, :BLOCK] * use[0] + near[index, c, :BLOCK, BLOCK:] * use[1]
                )

    factor = (2.0 * APER * BLOCK) ** (-0.5)
    for n in range(NC):
        for d in range(1, NZ):
            s3(n, d, lax.rem(z + d, NZ)).wait_recv()
        for k in range(NZ):
            for b in range(NBLK):
                for c in range(2):
                    far[n, c, b * BLOCK + k * SUB : b * BLOCK + (k + 1) * SUB] = gath[n, k, b, c]

        def product(index):
            rows = lhs[index].reshape(ROWS, NBLK * BLOCK)
            by_real = jnp.dot(rows, far[n, 0], preferred_element_type=F32)
            by_imag = jnp.dot(rows, far[n, 1], preferred_element_type=F32)
            real = by_real[:BLOCK] - by_imag[BLOCK:]
            imag = by_real[BLOCK:] + by_imag[:BLOCK]
            return (jnp.concatenate([real, imag], axis=0) * factor).astype(BF16)

        for d in range(1, NQ):
            index = lax.rem(q + d, NQ)
            stage[n, index] = product(index)
            o(n, d, q).start()
        out[:, columns(q, n)] = product(q)

    for n in range(NC):
        for d in range(1, NQ):
            o(n, d, lax.rem(q + d, NQ)).wait_recv()
    n1a.wait_send()
    n1b.wait_send()
    for d in range(1, NQ):
        n2(d, q).wait_send()
    for index in range(NQ):
        n3(index, core).wait_send()
    for n in range(NC):
        for e, d in offsets[n]:
            s1(n, e, d, q).wait_send()
        for d in range(1, NQ):
            o(n, d, q).wait_send()
        for d in range(1, NZ):
            s2(n, d, z).wait_send()
            s3(n, d, z).wait_send()


def per_device(records, aperture, block_owner, block_receivers):
    freqs, parts, shots_here, rcv_here = records.shape
    hbm = pl.BlockSpec(memory_space=pltpu.HBM)
    dma = pltpu.SemaphoreType.DMA
    out = pl.pallas_call(
        kernel,
        out_shape=jax.ShapeDtypeStruct((ROWS, rcv_here), BF16),
        in_specs=[hbm] * 4,
        out_specs=pl.BlockSpec(memory_space=pltpu.VMEM),
        scratch_shapes=[
            pltpu.VMEM((ROWS, NQ * SHARE), BF16),
            pltpu.VMEM((APER, BLOCK), jnp.int32),
            pltpu.VMEM((NBLK, BLOCK), jnp.int32),
            pltpu.SMEM((NBLK,), jnp.int32),
            pltpu.VMEM((2, NQ, BLOCK, LANES), BF16),
            pltpu.VMEM((2, NQ, BLOCK, LANES), BF16),
            pltpu.VMEM((NZ, NBLK, SUB, LANES), BF16),
            pltpu.VMEM((NZ, NBLK, SUB, LANES), BF16),
            pltpu.VMEM((NC, NZ, NBLK, SUB, LANES), BF16),
            pltpu.VMEM((NC, NBLK, 2, SUB, LANES), BF16),
            pltpu.VMEM((NC, NZ, NBLK, 2, SUB, LANES), BF16),
            pltpu.VMEM((NC, 2, NBLK * BLOCK, LANES), BF16),
            pltpu.VMEM((NQ, 2, BLOCK + TAIL, WIDTH), BF16),
            pltpu.VMEM((2, BLOCK, WIDTH), BF16),
            pltpu.VMEM((3, BLOCK, WIDTH), BF16),
            pltpu.VMEM((NQ, 2, BLOCK, NBLK * BLOCK), BF16),
            pltpu.VMEM((NC, NQ, ROWS, LANES), BF16),
            dma((4,)),
            dma((NC, 2, NQ)), dma((NC, 2, NQ)),
            dma((NC, NZ)), dma((NC, NZ)),
            dma((NC, NZ)), dma((NC, NZ)),
            dma((2,)), dma((2,)),
            dma((NQ,)), dma((NQ,)),
            dma((NQ,)), dma((NQ,)),
            dma((NC, NQ)), dma((NC, NQ)),
        ],
        compiler_params=pltpu.CompilerParams(
            collective_id=0, has_side_effects=True, vmem_limit_bytes=56 * 1024 * 1024
        ),
        cost_estimate=pl.CostEstimate(flops=2 * 10**9, bytes_accessed=2 * 2**20, transcendentals=0),
    )(records.reshape(ROWS, rcv_here), aperture.T, block_owner, block_receivers)
    return out.reshape(freqs, parts, shots_here, rcv_here)


def solution(mesh):
    placed = (P(None, None, "shot", "rcv"), P("shot", None), P(), P())
    return jax.shard_map(
        per_device,
        mesh=mesh,
        in_specs=placed,
        out_specs=P(None, None, "shot", "rcv"),
        check_vma=False,
    )
```

```python
import jax
import jax.numpy as jnp
from jax import lax
from jax.experimental import pallas as pl
from jax.experimental.pallas import tpu as pltpu
from jax.sharding import PartitionSpec as P

MESH = pl.DeviceIdType.MESH
BF16 = jnp.bfloat16
F32 = jnp.float32
APER = 2
BLOCK = 128
NBLK = 4
NX, NY, NZ, NR = 2, 4, 8, 4
NQ = NX * NY
SHARE = 256
NC = 2
LANES = SHARE // NC
ROWS = 2 * BLOCK
SUB = BLOCK // NZ
WIDTH = APER * BLOCK
TAIL = 16
SHIFT = (1, NZ - 1)


def remote(src, dst, send_sem, recv_sem, device):
    return pltpu.make_async_remote_copy(
        src_ref=src, dst_ref=dst, send_sem=send_sem, recv_sem=recv_sem, device_id=device, device_id_type=MESH
    )


def kernel(
    rec_hbm, ap_hbm, owner_hbm, recv_hbm, out,
    rec, ap, receivers, owner,
    scat0, scat1, zscat0, zscat1, sel, part, gath, far, near, local, given, lhs, stage,
    ins, s1s, s1r, s2s, s2r, s3s, s3r, n1s, n1r, n2s, n2r, n3s, n3r, os, orr,
):
    scat, zscat = (scat0, scat1), (zscat0, zscat1)
    shot, r = lax.axis_index("shot"), lax.axis_index("rcv")
    z, q = shot // NQ, lax.rem(shot, NQ)
    core = lax.rem(r, 2)
    other_core = (shot, r + 1 - 2 * core)
    other_x = (shot, lax.rem(r + 2, NR))

    inputs = [
        pltpu.make_async_copy(src, dst, ins.at[k])
        for k, (src, dst) in enumerate(((rec_hbm, rec), (ap_hbm, ap), (recv_hbm, receivers), (owner_hbm, owner)))
    ]
    for copy in inputs:
        copy.start()

    def at(index, plane):
        return (plane * NQ + index, r)

    def plane(d):
        index = lax.rem(q + d, NQ)
        return index, at(index, z)

    def line(d):
        index = lax.rem(z + d, NZ)
        return index, at(q, index)

    barrier = pltpu.get_barrier_semaphore()
    for d in range(1, NQ):
        index = lax.rem(q + d, NQ)
        for plane_of in (z, *(lax.rem(z + shift, NZ) for shift in SHIFT)):
            pl.semaphore_signal(barrier, inc=1, device_id=at(index, plane_of), device_id_type=MESH)
    for d in range(1, NZ):
        pl.semaphore_signal(barrier, inc=1, device_id=line(d)[1], device_id_type=MESH)
    pl.semaphore_signal(barrier, inc=1, device_id=other_core, device_id_type=MESH)
    pl.semaphore_signal(barrier, inc=1, device_id=other_x, device_id_type=MESH)
    for copy in inputs:
        copy.wait()
    pl.semaphore_wait(barrier, 3 * (NQ - 1) + NZ - 1 + 2)

    def columns(index, n):
        return pl.ds(pl.multiple_of(index * SHARE + n * LANES, LANES), LANES)

    def s1(n, e, d, source):
        index = lax.rem(q + d, NQ)
        return remote(
            rec.at[pl.ds(e * BLOCK, BLOCK), columns(index, n)], scat[n].at[e, source],
            s1s.at[n, e, d], s1r.at[n, e, source], at(index, lax.rem(z + e * SHIFT[n], NZ)),
        )

    def s2(n, d, source):
        index, device = line(d)
        return remote(sel.at[n, index], zscat[n].at[source], s2s.at[n, d], s2r.at[n, source], device)

    def s3(n, d, source):
        return remote(part.at[n], gath.at[n, source], s3s.at[n, d], s3r.at[n, source], line(d)[1])

    def o(n, d, source):
        index, device = plane(d)
        return remote(stage.at[n, index], out.at[:, columns(source, n)], os.at[n, d], orr.at[n, source], device)

    def own(n):
        return pltpu.make_async_copy(stage.at[n, q], out.at[:, columns(q, n)], ins.at[len(inputs) + n])

    def n2(d, source):
        return remote(near.at[q, core], near.at[source, core], n2s.at[d], n2r.at[source], plane(d)[1])

    def n3(index, half):
        return remote(near.at[index, half], near.at[index, half], n3s.at[index], n3r.at[index], other_core)

    offsets = [[(e, d) for d in range(NQ) for e in (1, 0) if (e, d) != (0, 0)]] * NC
    def scatter(n):
        for e, d in offsets[n]:
            s1(n, e, d, q).start()

    scatter(0)
    first = r * (NQ * SHARE)
    points = jnp.concatenate([receivers[b : b + 1, :] for b in range(NBLK)], axis=1)
    tile = 256
    total = jnp.zeros((ROWS, NBLK * BLOCK), F32)
    for k in range(NQ * SHARE // tile):
        ids = first + k * tile + lax.broadcasted_iota(jnp.int32, (tile, NBLK * BLOCK), 0)
        chosen = jnp.where(ids == points, 1.0, 0.0).astype(BF16)
        total += jnp.dot(rec[:, k * tile : (k + 1) * tile], chosen, preferred_element_type=F32)
    diagonal = lax.broadcasted_iota(jnp.int32, (BLOCK, BLOCK), 0) == lax.broadcasted_iota(
        jnp.int32, (BLOCK, BLOCK), 1
    )

    def upright(row):
        return jnp.sum(jnp.where(diagonal, row, 0.0), axis=1, keepdims=True)

    apertures = ap[...].astype(F32)
    for a in range(APER):
        block = upright(apertures[a : a + 1])
        for c in range(2):
            rows = total[c * BLOCK : (c + 1) * BLOCK]
            found = rows[:, :BLOCK]
            for b in range(1, NBLK):
                found = jnp.where(block == b, rows[:, b * BLOCK : (b + 1) * BLOCK], found)
            local[c, :, a * BLOCK : (a + 1) * BLOCK] = found.astype(BF16)

    n1a = remote(local.at[1 - core], given.at[0], n1s.at[0], n1r.at[0], other_core)
    n1a.start()
    for n in range(NC):
        scat[n][0, q] = rec[:BLOCK, columns(q, n)]
    tail = jnp.concatenate([apertures[a : a + 1] for a in range(APER)], axis=1)
    near[q, core, BLOCK:] = jnp.broadcast_to(tail, (TAIL, WIDTH)).astype(BF16)
    n1a.wait_recv()
    given[2] = local[core] + given[0]
    n1b = remote(given.at[2], given.at[1], n1s.at[1], n1r.at[1], other_x)
    n1b.start()
    scatter(1)

    zb = [owner[b] // NQ for b in range(NBLK)]
    qb = [lax.rem(owner[b], NQ) for b in range(NBLK)]

    def to_line(n):
        for e, d in offsets[n]:
            s1(n, e, d, lax.rem(q + d, NQ)).wait_recv()
        for b in range(NBLK):
            piece = scat[n][jnp.where(zb[b] == z, 0, 1), qb[b]]
            for k in range(NZ):
                sel[n, k, b] = piece[k * SUB : (k + 1) * SUB]
        for d in range(1, NZ):
            s2(n, d, z).start()
        zscat[n][z] = sel[n, z]

    def gather_line(n):
        for d in range(1, NZ):
            s2(n, d, lax.rem(z + d, NZ)).wait_recv()
        for b in range(NBLK):
            for c in range(2):
                part[n, b, c] = zscat[n][lax.rem(zb[b] + c * SHIFT[n], NZ), b]
        for d in range(1, NZ):
            s3(n, d, z).start()
        gath[n, z] = part[n]

    to_line(0)
    n1b.wait_recv()
    near[q, core, :BLOCK] = given[1] + given[2]
    for d in range(1, NQ):
        n2(d, q).start()
    n3(q, core).start()
    to_line(1)
    gather_line(0)
    for d in range(1, NQ):
        source = lax.rem(q + d, NQ)
        n2(d, source).wait_recv()
        n3(source, core).start()
    gather_line(1)
    for d in range(NQ):
        index = lax.rem(q + d, NQ)
        n3(index, 1 - core).wait_recv()
        tail = near[index, 0, BLOCK:].astype(F32)
        blocks = [upright(tail[:1, a * BLOCK : (a + 1) * BLOCK]) for a in range(APER)]
        for b in range(NBLK):
            use = [(block == b).astype(F32).astype(BF16) for block in blocks]
            for c in range(2):
                lhs[index, c, :, b * BLOCK : (b + 1) * BLOCK] = (
                    near[index, c, :BLOCK, :BLOCK] * use[0] + near[index, c, :BLOCK, BLOCK:] * use[1]
                )

    n1a.wait_send()
    n1b.wait_send()
    for d in range(1, NQ):
        n2(d, q).wait_send()
    for n in range(NC):
        for e, d in offsets[n]:
            s1(n, e, d, q).wait_send()
        for d in range(1, NZ):
            s2(n, d, z).wait_send()

    factor = (2.0 * APER * BLOCK) ** (-0.5)
    for n in range(NC):
        for d in range(1, NZ):
            s3(n, d, lax.rem(z + d, NZ)).wait_recv()
        for k in range(NZ):
            for b in range(NBLK):
                for c in range(2):
                    start = b * BLOCK + k * SUB
                    far[n, start : start + SUB, c * LANES : (c + 1) * LANES] = gath[n, k, b, c]

        def product(index):
            rows = lhs[index].reshape(ROWS, NBLK * BLOCK)
            both = jnp.dot(rows, far[n], preferred_element_type=F32)
            real = both[:BLOCK, :LANES] - both[BLOCK:, LANES:]
            imag = both[BLOCK:, :LANES] + both[:BLOCK, LANES:]
            return (jnp.concatenate([real, imag], axis=0) * factor).astype(BF16)

        for d in range(1, NQ):
            index = lax.rem(q + d, NQ)
            stage[n, index] = product(index)
            o(n, d, q).start()
        stage[n, q] = product(q)
        own(n).start()
        for d in range(1, NZ):
            s3(n, d, z).wait_send()
        if n == 0:
            for index in range(NQ):
                n3(index, core).wait_send()
        else:
            for d in range(1, NQ):
                o(n - 1, d, q).wait_send()

    for n in range(NC):
        own(n).wait()
        for d in range(1, NQ):
            o(n, d, lax.rem(q + d, NQ)).wait_recv()
    for d in range(1, NQ):
        o(NC - 1, d, q).wait_send()


def per_device(records, aperture, block_owner, block_receivers):
    freqs, parts, shots_here, rcv_here = records.shape
    hbm = pl.BlockSpec(memory_space=pltpu.HBM)
    dma = pltpu.SemaphoreType.DMA
    out = pl.pallas_call(
        kernel,
        out_shape=jax.ShapeDtypeStruct((ROWS, rcv_here), BF16),
        in_specs=[hbm] * 4,
        out_specs=hbm,
        scratch_shapes=[
            pltpu.VMEM((ROWS, NQ * SHARE), BF16),
            pltpu.VMEM((APER, BLOCK), jnp.int32),
            pltpu.VMEM((NBLK, BLOCK), jnp.int32),
            pltpu.SMEM((NBLK,), jnp.int32),
            pltpu.VMEM((2, NQ, BLOCK, LANES), BF16),
            pltpu.VMEM((2, NQ, BLOCK, LANES), BF16),
            pltpu.VMEM((NZ, NBLK, SUB, LANES), BF16),
            pltpu.VMEM((NZ, NBLK, SUB, LANES), BF16),
            pltpu.VMEM((NC, NZ, NBLK, SUB, LANES), BF16),
            pltpu.VMEM((NC, NBLK, 2, SUB, LANES), BF16),
            pltpu.VMEM((NC, NZ, NBLK, 2, SUB, LANES), BF16),
            pltpu.VMEM((NC, NBLK * BLOCK, 2 * LANES), BF16),
            pltpu.VMEM((NQ, 2, BLOCK + TAIL, WIDTH), BF16),
            pltpu.VMEM((2, BLOCK, WIDTH), BF16),
            pltpu.VMEM((3, BLOCK, WIDTH), BF16),
            pltpu.VMEM((NQ, 2, BLOCK, NBLK * BLOCK), BF16),
            pltpu.VMEM((NC, NQ, ROWS, LANES), BF16),
            dma((4 + NC,)),
            dma((NC, 2, NQ)), dma((NC, 2, NQ)),
            dma((NC, NZ)), dma((NC, NZ)),
            dma((NC, NZ)), dma((NC, NZ)),
            dma((2,)), dma((2,)),
            dma((NQ,)), dma((NQ,)),
            dma((NQ,)), dma((NQ,)),
            dma((NC, NQ)), dma((NC, NQ)),
        ],
        compiler_params=pltpu.CompilerParams(
            collective_id=0, has_side_effects=True, vmem_limit_bytes=56 * 1024 * 1024
        ),
        cost_estimate=pl.CostEstimate(flops=2 * 10**9, bytes_accessed=2 * 2**20, transcendentals=0),
    )(records.reshape(ROWS, rcv_here), aperture.T, block_owner, block_receivers)
    return out.reshape(freqs, parts, shots_here, rcv_here)


def solution(mesh):
    placed = (P(None, None, "shot", "rcv"), P("shot", None), P(), P())
    return jax.shard_map(
        per_device,
        mesh=mesh,
        in_specs=placed,
        out_specs=P(None, None, "shot", "rcv"),
        check_vma=False,
    )
```

```python
import jax
import jax.numpy as jnp
from jax import lax
from jax.experimental import pallas as pl
from jax.experimental.pallas import tpu as pltpu
from jax.sharding import PartitionSpec as P

MESH = pl.DeviceIdType.MESH
BF16 = jnp.bfloat16
F32 = jnp.float32
APER = 2
BLOCK = 128
NBLK = 4
NX, NY, NZ, NR = 2, 4, 8, 4
NQ = NX * NY
SHARE = 256
NC = 2
LANES = SHARE // NC
ROWS = 2 * BLOCK
SUB = BLOCK // NZ
WIDTH = APER * BLOCK
TAIL = 16
FAR_FIRST = ((0, 0), (1, 2), (1, 1), (1, 3), (0, 2), (1, 0), (0, 1), (0, 3))
LINE = (4, 3, 5, 2, 6, 1, 7)
SHIFT = (1, NZ - 1)


def remote(src, dst, send_sem, recv_sem, device):
    return pltpu.make_async_remote_copy(
        src_ref=src, dst_ref=dst, send_sem=send_sem, recv_sem=recv_sem, device_id=device, device_id_type=MESH
    )


def kernel(
    rec_hbm, ap_hbm, owner_hbm, recv_hbm, out,
    rec, ap, receivers, owner,
    scat0, scat1, zscat0, zscat1, sel, part, gath, far, near, local, given, lhs, stage,
    ins, s1s, s1r, s2s, s2r, s3s, s3r, n1s, n1r, n2s, n2r, n3s, n3r, os, orr,
):
    scat, zscat = (scat0, scat1), (zscat0, zscat1)
    shot, r = lax.axis_index("shot"), lax.axis_index("rcv")
    z, q = shot // NQ, lax.rem(shot, NQ)
    core = lax.rem(r, 2)
    other_core = (shot, r + 1 - 2 * core)
    other_x = (shot, lax.rem(r + 2, NR))

    inputs = [
        pltpu.make_async_copy(src, dst, ins.at[k])
        for k, (src, dst) in enumerate(((rec_hbm, rec), (ap_hbm, ap), (recv_hbm, receivers), (owner_hbm, owner)))
    ]
    for copy in inputs:
        copy.start()

    def at(index, plane):
        return (plane * NQ + index, r)

    def beside(d):
        dx, dy = FAR_FIRST[d]
        return lax.rem(q // NY + dx, NX) * NY + lax.rem(q + dy, NY)

    def plane(d):
        return beside(d), at(beside(d), z)

    def line(d):
        index = lax.rem(z + d, NZ)
        return index, at(q, index)

    barrier = pltpu.get_barrier_semaphore()
    for d in range(1, NQ):
        index = beside(d)
        for plane_of in (z, *(lax.rem(z + shift, NZ) for shift in SHIFT)):
            pl.semaphore_signal(barrier, inc=1, device_id=at(index, plane_of), device_id_type=MESH)
    for d in LINE:
        pl.semaphore_signal(barrier, inc=1, device_id=line(d)[1], device_id_type=MESH)
    pl.semaphore_signal(barrier, inc=1, device_id=other_core, device_id_type=MESH)
    pl.semaphore_signal(barrier, inc=1, device_id=other_x, device_id_type=MESH)
    for copy in inputs:
        copy.wait()
    pl.semaphore_wait(barrier, 3 * (NQ - 1) + NZ - 1 + 2)

    def columns(index, n):
        return pl.ds(pl.multiple_of(index * SHARE + n * LANES, LANES), LANES)

    def s1(n, e, d, source):
        index = beside(d)
        return remote(
            rec.at[pl.ds(e * BLOCK, BLOCK), columns(index, n)], scat[n].at[e, source],
            s1s.at[n, e, d], s1r.at[n, e, source], at(index, lax.rem(z + e * SHIFT[n], NZ)),
        )

    def s2(n, d, source):
        index, device = line(d)
        return remote(sel.at[n, index], zscat[n].at[source], s2s.at[n, d], s2r.at[n, source], device)

    def s3(n, d, source):
        return remote(part.at[n], gath.at[n, source], s3s.at[n, d], s3r.at[n, source], line(d)[1])

    def o(n, d, source):
        index, device = plane(d)
        return remote(stage.at[n, index], out.at[:, columns(source, n)], os.at[n, d], orr.at[n, source], device)

    def own(n):
        return pltpu.make_async_copy(stage.at[n, q], out.at[:, columns(q, n)], ins.at[len(inputs) + n])

    def n2(d, source):
        return remote(near.at[q, core], near.at[source, core], n2s.at[d], n2r.at[source], plane(d)[1])

    def n3(index, half):
        return remote(near.at[index, half], near.at[index, half], n3s.at[index], n3r.at[index], other_core)

    offsets = [[(e, d) for d in range(NQ) for e in (1, 0) if (e, d) != (0, 0)]] * NC
    def scatter(n):
        for e, d in offsets[n]:
            s1(n, e, d, q).start()

    scatter(0)
    first = r * (NQ * SHARE)
    points = jnp.concatenate([receivers[b : b + 1, :] for b in range(NBLK)], axis=1)
    tile = 256
    total = jnp.zeros((ROWS, NBLK * BLOCK), F32)
    for k in range(NQ * SHARE // tile):
        ids = first + k * tile + lax.broadcasted_iota(jnp.int32, (tile, NBLK * BLOCK), 0)
        chosen = jnp.where(ids == points, 1.0, 0.0).astype(BF16)
        total += jnp.dot(rec[:, k * tile : (k + 1) * tile], chosen, preferred_element_type=F32)
    diagonal = lax.broadcasted_iota(jnp.int32, (BLOCK, BLOCK), 0) == lax.broadcasted_iota(
        jnp.int32, (BLOCK, BLOCK), 1
    )

    def upright(row):
        return jnp.sum(jnp.where(diagonal, row, 0.0), axis=1, keepdims=True)

    apertures = ap[...].astype(F32)
    for a in range(APER):
        block = upright(apertures[a : a + 1])
        for c in range(2):
            rows = total[c * BLOCK : (c + 1) * BLOCK]
            found = rows[:, :BLOCK]
            for b in range(1, NBLK):
                found = jnp.where(block == b, rows[:, b * BLOCK : (b + 1) * BLOCK], found)
            local[c, :, a * BLOCK : (a + 1) * BLOCK] = found.astype(BF16)

    n1a = remote(local.at[1 - core], given.at[0], n1s.at[0], n1r.at[0], other_core)
    n1a.start()
    for n in range(NC):
        scat[n][0, q] = rec[:BLOCK, columns(q, n)]
    tail = jnp.concatenate([apertures[a : a + 1] for a in range(APER)], axis=1)
    near[q, core, BLOCK:] = jnp.broadcast_to(tail, (TAIL, WIDTH)).astype(BF16)
    n1a.wait_recv()
    given[2] = local[core] + given[0]
    n1b = remote(given.at[2], given.at[1], n1s.at[1], n1r.at[1], other_x)
    n1b.start()
    scatter(1)

    zb = [owner[b] // NQ for b in range(NBLK)]
    qb = [lax.rem(owner[b], NQ) for b in range(NBLK)]

    def to_line(n):
        for e, d in offsets[n]:
            s1(n, e, d, beside(d)).wait_recv()
        for b in range(NBLK):
            piece = scat[n][jnp.where(zb[b] == z, 0, 1), qb[b]]
            for k in range(NZ):
                sel[n, k, b] = piece[k * SUB : (k + 1) * SUB]
        for d in LINE:
            s2(n, d, z).start()
        zscat[n][z] = sel[n, z]

    def gather_line(n):
        for d in LINE:
            s2(n, d, lax.rem(z + d, NZ)).wait_recv()
        for b in range(NBLK):
            for c in range(2):
                part[n, b, c] = zscat[n][lax.rem(zb[b] + c * SHIFT[n], NZ), b]
        for d in LINE:
            s3(n, d, z).start()
        gath[n, z] = part[n]

    to_line(0)
    n1b.wait_recv()
    near[q, core, :BLOCK] = given[1] + given[2]
    for d in range(1, NQ):
        n2(d, q).start()
    n3(q, core).start()
    to_line(1)
    gather_line(0)
    for d in range(1, NQ):
        source = beside(d)
        n2(d, source).wait_recv()
        n3(source, core).start()
    gather_line(1)
    for d in range(NQ):
        index = beside(d)
        n3(index, 1 - core).wait_recv()
        tail = near[index, 0, BLOCK:].astype(F32)
        blocks = [upright(tail[:1, a * BLOCK : (a + 1) * BLOCK]) for a in range(APER)]
        for b in range(NBLK):
            use = [(block == b).astype(F32).astype(BF16) for block in blocks]
            for c in range(2):
                lhs[index, c, :, b * BLOCK : (b + 1) * BLOCK] = (
                    near[index, c, :BLOCK, :BLOCK] * use[0] + near[index, c, :BLOCK, BLOCK:] * use[1]
                )

    n1a.wait_send()
    n1b.wait_send()
    for d in range(1, NQ):
        n2(d, q).wait_send()
    for n in range(NC):
        for e, d in offsets[n]:
            s1(n, e, d, q).wait_send()
        for d in LINE:
            s2(n, d, z).wait_send()

    factor = (2.0 * APER * BLOCK) ** (-0.5)
    for n in range(NC):
        for d in LINE:
            s3(n, d, lax.rem(z + d, NZ)).wait_recv()
        for k in range(NZ):
            for b in range(NBLK):
                for c in range(2):
                    start = b * BLOCK + k * SUB
                    far[n, start : start + SUB, c * LANES : (c + 1) * LANES] = gath[n, k, b, c]

        def product(index):
            rows = lhs[index].reshape(ROWS, NBLK * BLOCK)
            both = jnp.dot(rows, far[n], preferred_element_type=F32)
            real = both[:BLOCK, :LANES] - both[BLOCK:, LANES:]
            imag = both[BLOCK:, :LANES] + both[:BLOCK, LANES:]
            return (jnp.concatenate([real, imag], axis=0) * factor).astype(BF16)

        for d in range(1, NQ):
            index = beside(d)
            stage[n, index] = product(index)
            o(n, d, q).start()
        stage[n, q] = product(q)
        own(n).start()
        for d in LINE:
            s3(n, d, z).wait_send()
        if n == 0:
            for index in range(NQ):
                n3(index, core).wait_send()
        else:
            for d in range(1, NQ):
                o(n - 1, d, q).wait_send()

    for n in range(NC):
        own(n).wait()
        for d in range(1, NQ):
            o(n, d, beside(d)).wait_recv()
    for d in range(1, NQ):
        o(NC - 1, d, q).wait_send()


def per_device(records, aperture, block_owner, block_receivers):
    freqs, parts, shots_here, rcv_here = records.shape
    hbm = pl.BlockSpec(memory_space=pltpu.HBM)
    dma = pltpu.SemaphoreType.DMA
    out = pl.pallas_call(
        kernel,
        out_shape=jax.ShapeDtypeStruct((ROWS, rcv_here), BF16),
        in_specs=[hbm] * 4,
        out_specs=hbm,
        scratch_shapes=[
            pltpu.VMEM((ROWS, NQ * SHARE), BF16),
            pltpu.VMEM((APER, BLOCK), jnp.int32),
            pltpu.VMEM((NBLK, BLOCK), jnp.int32),
            pltpu.SMEM((NBLK,), jnp.int32),
            pltpu.VMEM((2, NQ, BLOCK, LANES), BF16),
            pltpu.VMEM((2, NQ, BLOCK, LANES), BF16),
            pltpu.VMEM((NZ, NBLK, SUB, LANES), BF16),
            pltpu.VMEM((NZ, NBLK, SUB, LANES), BF16),
            pltpu.VMEM((NC, NZ, NBLK, SUB, LANES), BF16),
            pltpu.VMEM((NC, NBLK, 2, SUB, LANES), BF16),
            pltpu.VMEM((NC, NZ, NBLK, 2, SUB, LANES), BF16),
            pltpu.VMEM((NC, NBLK * BLOCK, 2 * LANES), BF16),
            pltpu.VMEM((NQ, 2, BLOCK + TAIL, WIDTH), BF16),
            pltpu.VMEM((2, BLOCK, WIDTH), BF16),
            pltpu.VMEM((3, BLOCK, WIDTH), BF16),
            pltpu.VMEM((NQ, 2, BLOCK, NBLK * BLOCK), BF16),
            pltpu.VMEM((NC, NQ, ROWS, LANES), BF16),
            dma((4 + NC,)),
            dma((NC, 2, NQ)), dma((NC, 2, NQ)),
            dma((NC, NZ)), dma((NC, NZ)),
            dma((NC, NZ)), dma((NC, NZ)),
            dma((2,)), dma((2,)),
            dma((NQ,)), dma((NQ,)),
            dma((NQ,)), dma((NQ,)),
            dma((NC, NQ)), dma((NC, NQ)),
        ],
        compiler_params=pltpu.CompilerParams(
            collective_id=0, has_side_effects=True, vmem_limit_bytes=56 * 1024 * 1024
        ),
        cost_estimate=pl.CostEstimate(flops=2 * 10**9, bytes_accessed=2 * 2**20, transcendentals=0),
    )(records.reshape(ROWS, rcv_here), aperture.T, block_owner, block_receivers)
    return out.reshape(freqs, parts, shots_here, rcv_here)


def solution(mesh):
    placed = (P(None, None, "shot", "rcv"), P("shot", None), P(), P())
    return jax.shard_map(
        per_device,
        mesh=mesh,
        in_specs=placed,
        out_specs=P(None, None, "shot", "rcv"),
        check_vma=False,
    )
```

```python
import jax
import jax.numpy as jnp
from jax import lax
from jax.experimental import pallas as pl
from jax.experimental.pallas import tpu as pltpu
from jax.sharding import PartitionSpec as P

MESH = pl.DeviceIdType.MESH
BF16 = jnp.bfloat16
F32 = jnp.float32
APER = 2
BLOCK = 128
NBLK = 4
NX, NY, NZ, NR = 2, 4, 8, 4
NQ = NX * NY
SHARE = 256
NC = 2
LANES = SHARE // NC
ROWS = 2 * BLOCK
SUB = BLOCK // NZ
WIDTH = APER * BLOCK
TAIL = 16
FAR_FIRST = ((0, 0), (1, 2), (1, 1), (1, 3), (0, 2), (1, 0), (0, 1), (0, 3))
LINE = (4, 3, 5, 2, 6, 1, 7)
SHIFT = (1, NZ - 1)


def remote(src, dst, send_sem, recv_sem, device):
    return pltpu.make_async_remote_copy(
        src_ref=src, dst_ref=dst, send_sem=send_sem, recv_sem=recv_sem, device_id=device, device_id_type=MESH
    )


def kernel(
    rec_hbm, ap_hbm, owner_hbm, recv_hbm, out,
    rec, ap, receivers, owner,
    scat0, scat1, zscat0, zscat1, sel, part, gath, far, near, local, given, lhs, stage,
    ins, s1s, s1r, s2s, s2r, s3s, s3r, n1s, n1r, n2s, n2r, n3s, n3r, os, orr,
):
    scat, zscat = (scat0, scat1), (zscat0, zscat1)
    shot, r = lax.axis_index("shot"), lax.axis_index("rcv")
    z, q = shot // NQ, lax.rem(shot, NQ)
    core = lax.rem(r, 2)
    other_core = (shot, r + 1 - 2 * core)
    other_x = (shot, lax.rem(r + 2, NR))

    inputs = [
        pltpu.make_async_copy(src, dst, ins.at[k])
        for k, (src, dst) in enumerate(((rec_hbm, rec), (ap_hbm, ap), (recv_hbm, receivers), (owner_hbm, owner)))
    ]
    for copy in inputs:
        copy.start()

    def at(index, plane):
        return (plane * NQ + index, r)

    def beside(d):
        dx, dy = FAR_FIRST[d]
        return lax.rem(q // NY + dx, NX) * NY + lax.rem(q + dy, NY)

    def plane(d):
        return beside(d), at(beside(d), z)

    def line(d):
        index = lax.rem(z + d, NZ)
        return index, at(q, index)

    barrier = pltpu.get_barrier_semaphore()
    steps = [(d, shift) for d in range(1, NQ) for shift in (0, *SHIFT)] + [(0, shift) for shift in LINE]
    hops = {d: dx + min(dy, NY - dy) for d, (dx, dy) in enumerate(FAR_FIRST)}
    for d, shift in sorted(steps, key=lambda step: -(hops[step[0]] + min(step[1], NZ - step[1]))):
        device = at(beside(d), lax.rem(z + shift, NZ))
        pl.semaphore_signal(barrier, inc=1, device_id=device, device_id_type=MESH)
    pl.semaphore_signal(barrier, inc=1, device_id=other_core, device_id_type=MESH)
    pl.semaphore_signal(barrier, inc=1, device_id=other_x, device_id_type=MESH)
    for copy in inputs:
        copy.wait()
    pl.semaphore_wait(barrier, 3 * (NQ - 1) + NZ - 1 + 2)

    def columns(index, n):
        return pl.ds(pl.multiple_of(index * SHARE + n * LANES, LANES), LANES)

    def s1(n, e, d, source):
        index = beside(d)
        return remote(
            rec.at[pl.ds(e * BLOCK, BLOCK), columns(index, n)], scat[n].at[e, source],
            s1s.at[n, e, d], s1r.at[n, e, source], at(index, lax.rem(z + e * SHIFT[n], NZ)),
        )

    def s2(n, d, source):
        index, device = line(d)
        return remote(sel.at[n, index], zscat[n].at[source], s2s.at[n, d], s2r.at[n, source], device)

    def s3(n, d, source):
        return remote(part.at[n], gath.at[n, source], s3s.at[n, d], s3r.at[n, source], line(d)[1])

    def o(n, d, source):
        index, device = plane(d)
        return remote(stage.at[n, index], out.at[:, columns(source, n)], os.at[n, d], orr.at[n, source], device)

    def own(n):
        return pltpu.make_async_copy(stage.at[n, q], out.at[:, columns(q, n)], ins.at[len(inputs) + n])

    def n2(d, source):
        return remote(near.at[q, core], near.at[source, core], n2s.at[d], n2r.at[source], plane(d)[1])

    def n3(index, half):
        return remote(near.at[index, half], near.at[index, half], n3s.at[index], n3r.at[index], other_core)

    offsets = [[(e, d) for d in range(NQ) for e in (1, 0) if (e, d) != (0, 0)]] * NC
    def scatter(n):
        for e, d in offsets[n]:
            s1(n, e, d, q).start()

    scatter(0)
    first = r * (NQ * SHARE)
    points = jnp.concatenate([receivers[b : b + 1, :] for b in range(NBLK)], axis=1)
    tile = 256
    total = jnp.zeros((ROWS, NBLK * BLOCK), F32)
    for k in range(NQ * SHARE // tile):
        ids = first + k * tile + lax.broadcasted_iota(jnp.int32, (tile, NBLK * BLOCK), 0)
        chosen = jnp.where(ids == points, 1.0, 0.0).astype(BF16)
        total += jnp.dot(rec[:, k * tile : (k + 1) * tile], chosen, preferred_element_type=F32)
    diagonal = lax.broadcasted_iota(jnp.int32, (BLOCK, BLOCK), 0) == lax.broadcasted_iota(
        jnp.int32, (BLOCK, BLOCK), 1
    )

    def upright(row):
        return jnp.sum(jnp.where(diagonal, row, 0.0), axis=1, keepdims=True)

    apertures = ap[...].astype(F32)
    for a in range(APER):
        block = upright(apertures[a : a + 1])
        for c in range(2):
            rows = total[c * BLOCK : (c + 1) * BLOCK]
            found = rows[:, :BLOCK]
            for b in range(1, NBLK):
                found = jnp.where(block == b, rows[:, b * BLOCK : (b + 1) * BLOCK], found)
            local[c, :, a * BLOCK : (a + 1) * BLOCK] = found.astype(BF16)

    n1a = remote(local.at[1 - core], given.at[0], n1s.at[0], n1r.at[0], other_core)
    n1a.start()
    for n in range(NC):
        scat[n][0, q] = rec[:BLOCK, columns(q, n)]
    tail = jnp.concatenate([apertures[a : a + 1] for a in range(APER)], axis=1)
    near[q, core, BLOCK:] = jnp.broadcast_to(tail, (TAIL, WIDTH)).astype(BF16)
    n1a.wait_recv()
    given[2] = local[core] + given[0]
    n1b = remote(given.at[2], given.at[1], n1s.at[1], n1r.at[1], other_x)
    n1b.start()
    scatter(1)

    zb = [owner[b] // NQ for b in range(NBLK)]
    qb = [lax.rem(owner[b], NQ) for b in range(NBLK)]

    def to_line(n):
        for e, d in offsets[n]:
            s1(n, e, d, beside(d)).wait_recv()
        for b in range(NBLK):
            piece = scat[n][jnp.where(zb[b] == z, 0, 1), qb[b]]
            for k in range(NZ):
                sel[n, k, b] = piece[k * SUB : (k + 1) * SUB]
        for d in LINE:
            s2(n, d, z).start()
        zscat[n][z] = sel[n, z]

    def gather_line(n):
        for d in LINE:
            s2(n, d, lax.rem(z + d, NZ)).wait_recv()
        for b in range(NBLK):
            for c in range(2):
                part[n, b, c] = zscat[n][lax.rem(zb[b] + c * SHIFT[n], NZ), b]
        for d in LINE:
            s3(n, d, z).start()
        gath[n, z] = part[n]

    to_line(0)
    n1b.wait_recv()
    near[q, core, :BLOCK] = given[1] + given[2]
    for d in range(1, NQ):
        n2(d, q).start()
    n3(q, core).start()
    to_line(1)
    gather_line(0)
    for d in range(1, NQ):
        source = beside(d)
        n2(d, source).wait_recv()
        n3(source, core).start()
    gather_line(1)
    for d in range(NQ):
        index = beside(d)
        n3(index, 1 - core).wait_recv()
        tail = near[index, 0, BLOCK:].astype(F32)
        blocks = [upright(tail[:1, a * BLOCK : (a + 1) * BLOCK]) for a in range(APER)]
        for b in range(NBLK):
            use = [(block == b).astype(F32).astype(BF16) for block in blocks]
            for c in range(2):
                lhs[index, c, :, b * BLOCK : (b + 1) * BLOCK] = (
                    near[index, c, :BLOCK, :BLOCK] * use[0] + near[index, c, :BLOCK, BLOCK:] * use[1]
                )

    n1a.wait_send()
    n1b.wait_send()
    for d in range(1, NQ):
        n2(d, q).wait_send()
    for n in range(NC):
        for e, d in offsets[n]:
            s1(n, e, d, q).wait_send()
        for d in LINE:
            s2(n, d, z).wait_send()

    factor = (2.0 * APER * BLOCK) ** (-0.5)
    for n in range(NC):
        for d in LINE:
            s3(n, d, lax.rem(z + d, NZ)).wait_recv()
        for k in range(NZ):
            for b in range(NBLK):
                for c in range(2):
                    start = b * BLOCK + k * SUB
                    far[n, start : start + SUB, c * LANES : (c + 1) * LANES] = gath[n, k, b, c]

        def product(index):
            rows = lhs[index].reshape(ROWS, NBLK * BLOCK)
            both = jnp.dot(rows, far[n], preferred_element_type=F32)
            real = both[:BLOCK, :LANES] - both[BLOCK:, LANES:]
            imag = both[BLOCK:, :LANES] + both[:BLOCK, LANES:]
            return (jnp.concatenate([real, imag], axis=0) * factor).astype(BF16)

        for d in range(1, NQ):
            index = beside(d)
            stage[n, index] = product(index)
            o(n, d, q).start()
        stage[n, q] = product(q)
        own(n).start()
        for d in LINE:
            s3(n, d, z).wait_send()
        if n == 0:
            for index in range(NQ):
                n3(index, core).wait_send()
        else:
            for d in range(1, NQ):
                o(n - 1, d, q).wait_send()

    for n in range(NC):
        own(n).wait()
        for d in range(1, NQ):
            o(n, d, beside(d)).wait_recv()
    for d in range(1, NQ):
        o(NC - 1, d, q).wait_send()


def per_device(records, aperture, block_owner, block_receivers):
    freqs, parts, shots_here, rcv_here = records.shape
    hbm = pl.BlockSpec(memory_space=pltpu.HBM)
    dma = pltpu.SemaphoreType.DMA
    out = pl.pallas_call(
        kernel,
        out_shape=jax.ShapeDtypeStruct((ROWS, rcv_here), BF16),
        in_specs=[hbm] * 4,
        out_specs=hbm,
        scratch_shapes=[
            pltpu.VMEM((ROWS, NQ * SHARE), BF16),
            pltpu.VMEM((APER, BLOCK), jnp.int32),
            pltpu.VMEM((NBLK, BLOCK), jnp.int32),
            pltpu.SMEM((NBLK,), jnp.int32),
            pltpu.VMEM((2, NQ, BLOCK, LANES), BF16),
            pltpu.VMEM((2, NQ, BLOCK, LANES), BF16),
            pltpu.VMEM((NZ, NBLK, SUB, LANES), BF16),
            pltpu.VMEM((NZ, NBLK, SUB, LANES), BF16),
            pltpu.VMEM((NC, NZ, NBLK, SUB, LANES), BF16),
            pltpu.VMEM((NC, NBLK, 2, SUB, LANES), BF16),
            pltpu.VMEM((NC, NZ, NBLK, 2, SUB, LANES), BF16),
            pltpu.VMEM((NC, NBLK * BLOCK, 2 * LANES), BF16),
            pltpu.VMEM((NQ, 2, BLOCK + TAIL, WIDTH), BF16),
            pltpu.VMEM((2, BLOCK, WIDTH), BF16),
            pltpu.VMEM((3, BLOCK, WIDTH), BF16),
            pltpu.VMEM((NQ, 2, BLOCK, NBLK * BLOCK), BF16),
            pltpu.VMEM((NC, NQ, ROWS, LANES), BF16),
            dma((4 + NC,)),
            dma((NC, 2, NQ)), dma((NC, 2, NQ)),
            dma((NC, NZ)), dma((NC, NZ)),
            dma((NC, NZ)), dma((NC, NZ)),
            dma((2,)), dma((2,)),
            dma((NQ,)), dma((NQ,)),
            dma((NQ,)), dma((NQ,)),
            dma((NC, NQ)), dma((NC, NQ)),
        ],
        compiler_params=pltpu.CompilerParams(
            collective_id=0, has_side_effects=True, vmem_limit_bytes=56 * 1024 * 1024
        ),
        cost_estimate=pl.CostEstimate(flops=2 * 10**9, bytes_accessed=2 * 2**20, transcendentals=0),
    )(records.reshape(ROWS, rcv_here), aperture.T, block_owner, block_receivers)
    return out.reshape(freqs, parts, shots_here, rcv_here)


def solution(mesh):
    placed = (P(None, None, "shot", "rcv"), P("shot", None), P(), P())
    return jax.shard_map(
        per_device,
        mesh=mesh,
        in_specs=placed,
        out_specs=P(None, None, "shot", "rcv"),
        check_vma=False,
    )
```
